32 devices in a mesh: groups: 2 (over y), etp: 4 (over x, core), expert: 4 (over z).
Axes of the slice: x: 2, y: 2, z: 4, core: 2. Of those that a mesh axis runs over, the one named last changes fastest.
Arguments:
- tokens: bfloat16 [1024, 3072], P(('groups', 'expert')), parts along dimension 0, may hold values from -6 to 6
- expert_ids: int32 [1024, 2], P(('groups', 'expert')), parts along dimension 0, may hold values from 0 to 3, as said below
- route_weights: float32 [1024, 2], P(('groups', 'expert')), parts along dimension 0, may hold values from 0.1 to 1
- w_gate: bfloat16 [4, 3072, 8192], P('expert', None, 'etp'), may hold values from -0.109375 to 0.109375
- w_up: bfloat16 [4, 3072, 8192], P('expert', None, 'etp'), may hold values from -0.109375 to 0.109375
- w_down: bfloat16 [4, 8192, 3072], P('expert', 'etp'), may hold values from -0.09375 to 0.09375
Outputs:
- layer_out: bfloat16 [1024, 3072], P(('groups', 'expert'), 'etp'), parts along dimension 0
The draws below stay inside these ranges and needn't reach their ends.
There are 2 independent parts, one for each index of `groups`. The reference program is written for one: setup_inputs(seed, part) draws one part's arguments, and reference() takes and returns one part's arrays. A program takes and returns all parts, laid end to end along the dimension named above; an argument that names none is the same for every part. Nothing has to cross between parts.
Inputs may be any that keep to these rules, and one draw needn't show every extreme that they name: `expert_ids`: the two experts of a token differ. In each aligned block of 128 rows no expert is named by more than 80 rows, and one expert, the same in all blocks of a part, is named by exactly 80 rows in every block.
All inputs are finite; a program needn't handle non-finite values.
Results may differ from the reference program's by a relative error of at most 0.01.
Values may be sent and summed in bfloat16 or wider, within the bound.
A program may use at most 128 MiB of HBM per device.

```python
import math
import jax
import jax.numpy as jnp
from jax import lax

D = 3072
FF = 8192
EXPERTS = 4
TOPK = 2
TOK_DEV = 128
CAP = 80
TOKENS = 512
N_ETP = 4


def draw_expert_ids(key, part):
    key = jax.random.fold_in(key, 11)
    key_hot, key_blocks = jax.random.split(key, 2)
    hottest = jax.random.randint(key_hot, (), 0, EXPERTS)
    capacity = TOK_DEV * 5 // 8

    def relabel(index):
        return index + (index >= hottest).astype(jnp.int32)

    def one_block(block_key):
        key_order, key_shift, key_offset = jax.random.split(block_key, 3)
        order = jax.random.permutation(key_order, TOK_DEV)
        ranks = jnp.argsort(order).astype(jnp.int32)
        shift = jax.random.randint(key_shift, (), 0, EXPERTS - 2)
        offset = jax.random.randint(key_offset, (), 0, EXPERTS - 1)
        second_index = (ranks + offset) % (EXPERTS - 1)
        first_index = (ranks + offset + 1 + shift) % (EXPERTS - 1)
        first = jnp.where(ranks < capacity, hottest, relabel(first_index))
        second = relabel(second_index)
        return jnp.stack([first, second], axis=-1)
    block_keys = jax.random.split(key_blocks, EXPERTS)
    chosen = jax.vmap(one_block)(block_keys)
    return chosen.reshape(TOKENS, 2).astype(jnp.int32)


def spiked(entries, key, source, target, shards_of, factor):
    def block_of(axis_at):
        return (jnp.arange(entries.shape[axis_at]) // (entries.shape[axis_at] // shards_of)).reshape((-1,) + (1,) * (entries.ndim - 1 - axis_at))

    first = jax.random.permutation(key, shards_of)[block_of(target)]
    other_side = (block_of(target) + shards_of // 2) % shards_of
    return jnp.where((block_of(source) == first) | (block_of(source) == other_side), factor * entries, entries)


def block_scale(own_key, dims, shards, smallest, largest):
    def one(dim, shards_of):
        draws = jax.random.uniform(jax.random.fold_in(jax.random.fold_in(own_key, 6), dim), (shards_of,), jnp.float32, smallest / len(shards), largest / len(shards))
        return jnp.repeat(jnp.exp(draws), dims[dim] // shards_of).reshape((-1,) + (1,) * (len(dims) - dim - 1))

    gain = one(*shards[0])
    for cut in shards[1:]:
        gain = gain * one(*cut)
    return gain


def normal_values(stream_key, extent, width, reach, cuts=(), held_as=jnp.bfloat16):
    loudness = block_scale(stream_key, extent, cuts, -0.22, 0.18) if cuts else 1.0
    values = jax.random.normal(stream_key, extent, jnp.float32) * width * loudness
    return jnp.minimum(jnp.maximum(values, -reach), reach).astype(held_as)


def bell_draw_with(rng, dims, spread, reach, shards, heavy, kind=jnp.bfloat16):
    values = spread * jax.random.normal(rng, dims, jnp.float32)
    if shards:
        values = values * block_scale(rng, dims, shards, -0.22, 0.18)
    return jnp.clip(spiked(values, jax.random.fold_in(rng, 3), *heavy), -reach, reach).astype(kind)


def setup_inputs(seed: int = 0, part: int = 0) -> dict:
    seeds = jax.random.split(jax.random.key(seed), 7)
    own_keys = jax.random.split(jax.random.fold_in(seeds[6], part), 7)
    tokens = normal_values(own_keys[0], (TOKENS, D), 1.0, 6.0, ((0, 4),))
    expert_ids = draw_expert_ids(jax.random.fold_in(jax.random.fold_in(seeds[6], part), 71), part)
    route_weights = jnp.clip(jnp.exp(math.log(1.0) - 2.3025851 * jax.random.uniform(own_keys[2], (TOKENS, TOPK), jnp.float32) ** block_scale(own_keys[2], (TOKENS, TOPK), ((0, 4),), -0.2, 0.2)), 0.1, 1.0)
    w_gate = normal_values(seeds[3], (EXPERTS, D, FF), D ** -0.5, 0.109375, ((0, 4), (2, 4)))
    w_up = normal_values(seeds[4], (EXPERTS, D, FF), D ** -0.5, 0.109375, ((0, 4), (2, 4)))
    w_down = bell_draw_with(seeds[5], (EXPERTS, FF, D), FF ** -0.5, 0.09375, ((0, 4), (1, 4)), (1, 2, 4, 2.0))
    return {"tokens": tokens, "expert_ids": expert_ids, "route_weights": route_weights, "w_gate": w_gate, "w_up": w_up, "w_down": w_down}


def expert_block(rows_in, gate_w, up_w, down_w):
    gate_act = jnp.dot(rows_in, gate_w, preferred_element_type=jnp.float32)
    up_act = jnp.dot(rows_in, up_w, preferred_element_type=jnp.float32)
    hidden = (jax.nn.silu(gate_act) * up_act).astype(jnp.bfloat16)
    count_rows = rows_in.shape[0]
    piece_width = FF // N_ETP
    pieces = hidden.reshape(count_rows, N_ETP, piece_width).astype(jnp.float32)
    down_pieces = down_w.reshape(N_ETP, piece_width, D).astype(jnp.float32)
    partial_value = jnp.einsum("rnf,nfd->nrd", pieces, down_pieces)
    rounded = lax.optimization_barrier(partial_value.astype(jnp.bfloat16)).astype(jnp.float32)
    return jnp.sum(rounded, axis=0).astype(jnp.bfloat16)


def reference(tokens, expert_ids, route_weights, w_gate, w_up, w_down):
    routes = expert_ids.reshape(EXPERTS, TOK_DEV * 2).astype(jnp.int32)
    labels = jnp.arange(EXPERTS, dtype=jnp.int32)
    matches = (routes[:, :, None] == labels[None, None, :]).astype(jnp.int32)
    earlier = jnp.cumsum(matches, axis=1) - matches
    slots = jnp.sum(earlier * matches, axis=2).astype(jnp.int32)
    sources = jnp.broadcast_to(labels[:, None], routes.shape)
    token_rows = jnp.repeat(tokens.reshape(EXPERTS, TOK_DEV, D), 2, axis=1)
    buffers = jnp.zeros((EXPERTS, EXPERTS, CAP, D), tokens.dtype).at[routes, sources, slots].set(token_rows)

    def one_expert(operands):
        block, gate_w, up_w, down_w = operands
        result = expert_block(block.reshape(EXPERTS * CAP, D), gate_w, up_w, down_w)
        return result.reshape(EXPERTS, CAP, D)

    outputs = lax.map(one_expert, (buffers, w_gate, w_up, w_down))
    picked = outputs[routes, sources, slots].astype(jnp.float32)
    weighted = picked * route_weights.reshape(EXPERTS, TOK_DEV * 2)[:, :, None]
    summed = jnp.sum(weighted.reshape(EXPERTS, TOK_DEV, 2, D), axis=2)
    return summed.astype(jnp.bfloat16).reshape(TOKENS, D)
```

```python
import functools

import jax
import jax.numpy as jnp
from jax import lax
from jax.experimental import pallas as pl
from jax.experimental.pallas import tpu as pltpu
from jax.sharding import PartitionSpec as P

MESH = pl.DeviceIdType.MESH
F32 = jnp.float32
BF16 = jnp.bfloat16
TILE = 256
PARTS = 4


def route_places(expert_ids, experts, capacity):
    routes_flat = expert_ids.reshape(-1)
    labels = jnp.arange(experts, dtype=jnp.int32)
    matches = (routes_flat[:, None] == labels[None, :]).astype(jnp.int32)
    earlier = jnp.cumsum(matches, axis=0) - matches
    slots = jnp.sum(earlier * matches, axis=1)
    return routes_flat * capacity + slots


def dispatch_rows(source_rows, places, experts, capacity):
    count_rows = source_rows.shape[0]
    targets = jnp.arange(experts * capacity, dtype=jnp.int32)
    matrix = (targets[:, None] == places[None, :]).astype(BF16)
    matrix = matrix.reshape(experts * capacity, count_rows, 2).sum(axis=2)
    placed = jnp.dot(matrix, source_rows, preferred_element_type=F32).astype(BF16)
    return placed.reshape(experts, capacity, source_rows.shape[1])


def wide_body(tokens, expert_ids, route_weights, w_gate, w_up, w_down):
    experts = lax.axis_size("expert")
    shards = lax.axis_size("etp")
    tok_rows = tokens.shape[0]
    capacity = tok_rows * 5 // 8
    model_width = tokens.shape[1]
    slice_width = model_width // shards
    places = route_places(expert_ids, experts, capacity)
    outgoing = dispatch_rows(tokens, places, experts, capacity)
    arrived = lax.all_to_all(outgoing, "expert", split_axis=0, concat_axis=0, tiled=True)
    rows_in = arrived.reshape(experts * capacity, model_width)
    gate_act = jnp.dot(rows_in, w_gate[0], preferred_element_type=F32)
    up_act = jnp.dot(rows_in, w_up[0], preferred_element_type=F32)
    hidden = (jax.nn.silu(gate_act) * up_act).astype(BF16)
    partial_rows = jnp.dot(hidden, w_down[0], preferred_element_type=F32).astype(BF16)
    partial_value = partial_rows.reshape(experts, capacity, model_width)
    expert_out = lax.psum_scatter(partial_value, "etp", scatter_dimension=2, tiled=True)
    returned = lax.all_to_all(expert_out, "expert", split_axis=0, concat_axis=0, tiled=True)
    picked = returned.reshape(experts * capacity, slice_width)[places]
    weighted = picked.astype(F32) * route_weights.reshape(-1)[:, None]
    combined = jnp.sum(weighted.reshape(tok_rows, 2, slice_width), axis=1)
    return combined.astype(BF16)


def layer_kernel(
    experts,
    ids_ref, wts_ref, tok_ref, gate_hbm, up_hbm, down_hbm,
    out_ref,
    gate, up, down, rows, outgoing, hidden, mix,
    core_out, core_in, far_sum, own_sum, x_out, x_in, z_out, returned,
    w_sem, z_send, z_recv, c_send, c_recv, x_send, x_recv, d_send, d_recv,
    pc_send, pc_recv, px_send, px_recv, pz_send, pz_recv,
):
    me = lax.axis_index("etp")
    z = lax.axis_index("expert")
    chip = me // 2
    core = me - chip * 2
    core_peer = chip * 2 + (1 - core)
    x_peer = (1 - chip) * 2 + core
    diagonal = (1 - chip) * 2 + (1 - core)
    tok_rows = tok_ref.shape[0]
    cap = rows.shape[2]
    width = rows.shape[3]
    total = experts * cap
    units = hidden.shape[1]

    in_chunk = gate.shape[0] // PARTS
    down_chunk = down.shape[0] // PARTS
    weight_copies = []
    for part in range(PARTS):
        at = slice(part * in_chunk, (part + 1) * in_chunk)
        weight_copies.append(pltpu.make_async_copy(gate_hbm.at[0, at], gate.at[at], w_sem.at[0, part]))
        weight_copies.append(pltpu.make_async_copy(up_hbm.at[0, at], up.at[at], w_sem.at[1, part]))
    for part in range(PARTS):
        at = slice(part * down_chunk, (part + 1) * down_chunk)
        weight_copies.append(pltpu.make_async_copy(down_hbm.at[0, at], down.at[at], w_sem.at[2, part]))
    for copy in weight_copies:
        copy.start()

    barrier = pltpu.get_barrier_semaphore()
    others = [lax.rem(z + d, experts) for d in range(experts)]
    for d in range(1, experts):
        pl.semaphore_signal(barrier, inc=1, device_id={"expert": others[d]}, device_id_type=MESH)
    for peer in (core_peer, x_peer):
        pl.semaphore_signal(barrier, inc=1, device_id={"etp": peer}, device_id_type=MESH)

    ids = ids_ref[...]
    lane = lax.broadcasted_iota(jnp.int32, (tok_rows, 128), 1)
    match = [ids[:, k : k + 1] == lane for k in range(2)]
    counts = (match[0].astype(F32) + match[1].astype(F32)).astype(BF16)
    row_at = lax.broadcasted_iota(jnp.int32, (tok_rows, tok_rows), 0)
    col_at = lax.broadcasted_iota(jnp.int32, (tok_rows, tok_rows), 1)
    before = (col_at < row_at).astype(F32).astype(BF16)
    earlier = jnp.dot(before, counts, preferred_element_type=F32)
    places = []
    for k in range(2):
        slot = jnp.sum(jnp.where(match[k], earlier, 0.0), axis=1, keepdims=True)
        places.append(ids[:, k : k + 1] * cap + slot.astype(jnp.int32))
    target = lax.broadcasted_iota(jnp.int32, (tok_rows, total), 1)
    hit = [places[k] == target for k in range(2)]
    wts = wts_ref[...]
    mix[...] = jnp.where(hit[0], wts[:, 0:1], 0.0) + jnp.where(hit[1], wts[:, 1:2], 0.0)
    spread = (hit[0].astype(F32) + hit[1].astype(F32)).astype(BF16)
    first_dims = (((0,), (0,)), ((), ()))
    my_columns = tok_ref[:, pl.ds(pl.multiple_of(me * width, 128), width)]
    placed = lax.dot_general(spread, my_columns, first_dims, preferred_element_type=F32)
    outgoing[...] = placed.astype(BF16).reshape(experts, cap, width)

    pl.semaphore_wait(barrier, experts + 1)

    def remote(src, dst, send, recv, **device):
        return pltpu.make_async_remote_copy(
            src_ref=src, dst_ref=dst, send_sem=send, recv_sem=recv,
            device_id=device, device_id_type=MESH,
        )

    sent = []

    def go(copy):
        copy.start()
        sent.append(copy)
        return copy

    z_copies = [
        go(remote(outgoing.at[others[d]], rows.at[me, z], z_send.at[d], z_recv.at[d], expert=others[d]))
        for d in range(1, experts)
    ]

    wide = lax.broadcasted_iota(jnp.int32, (tok_rows, 128), 1)
    own_hit = [(places[k] - z * cap == wide) & (wide < cap) for k in range(2)]
    own_spread = (own_hit[0].astype(F32) + own_hit[1].astype(F32)).astype(BF16)
    for q in range(PARTS):
        own = lax.dot_general(
            own_spread, tok_ref[:, q * width : (q + 1) * width], first_dims, preferred_element_type=F32
        )
        rows[q, z] = own[:cap].astype(BF16)

    c_copies, x_copies, d_copies = [], [], []
    for d in range(1, experts):
        source = lax.rem(z + experts - d, experts)
        z_copies[d - 1].wait_recv()
        block = rows.at[me, source]
        x_copies.append(go(remote(block, block, x_send.at[d], x_recv.at[d], etp=x_peer)))
        c_copies.append(go(remote(block, block, c_send.at[d], c_recv.at[d], etp=core_peer)))
    for d in range(1, experts):
        source = lax.rem(z + experts - d, experts)
        x_copies[d - 1].wait_recv()
        block = rows.at[x_peer, source]
        d_copies.append(go(remote(block, block, d_send.at[d], d_recv.at[d], etp=core_peer)))
    for copy in weight_copies[: 2 * PARTS]:
        copy.wait()
    for d in range(1, experts):
        c_copies[d - 1].wait_recv()
        d_copies[d - 1].wait_recv()

    @pl.loop(0, units // TILE)
    def _(n):
        cols = pl.ds(pl.multiple_of(n * TILE, TILE), TILE)
        gate_act = jnp.zeros((total, TILE), F32)
        up_act = jnp.zeros((total, TILE), F32)
        for q in range(PARTS):
            block = rows[q].reshape(total, width)
            at = slice(q * width, (q + 1) * width)
            gate_act += jnp.dot(block, gate[at, cols], preferred_element_type=F32)
            up_act += jnp.dot(block, up[at, cols], preferred_element_type=F32)
        hidden[:, cols] = (gate_act / (1.0 + jnp.exp(-gate_act)) * up_act).astype(BF16)

    for copy in weight_copies[2 * PARTS :]:
        copy.wait()

    def project(q, target_ref):
        @pl.loop(0, width // TILE)
        def _(n):
            start = pl.multiple_of(n * TILE, TILE)
            cols = pl.ds(pl.multiple_of(q * width + n * TILE, TILE), TILE)
            value = jnp.dot(hidden[...], down[:, cols], preferred_element_type=F32)
            target_ref[:, :, pl.ds(start, TILE)] = value.reshape(experts, cap, TILE).astype(target_ref.dtype)

    project(diagonal, core_out.at[0])
    first = go(remote(core_out.at[0], core_in.at[0], pc_send.at[0], pc_recv.at[0], etp=core_peer))
    project(x_peer, far_sum)
    first.wait_recv()
    px = []
    order = [others[d] for d in range(1, experts)] + [z]
    for i, block in enumerate(order):
        x_out[block] = (far_sum[block] + core_in[0, block].astype(F32)).astype(BF16)
        px.append(go(remote(x_out.at[block], x_in.at[block], px_send.at[i], px_recv.at[i], etp=x_peer)))
    project(core_peer, core_out.at[1])
    second = go(remote(core_out.at[1], core_in.at[1], pc_send.at[1], pc_recv.at[1], etp=core_peer))
    project(me, own_sum)
    second.wait_recv()

    pz = []
    for i, block in enumerate(order):
        px[i].wait_recv()
        value = own_sum[block] + core_in[1, block].astype(F32) + x_in[block].astype(F32)
        if i < experts - 1:
            z_out[block] = value.astype(BF16)
            pz.append(go(remote(z_out.at[block], returned.at[z], pz_send.at[i], pz_recv.at[i], expert=block)))
        else:
            returned[z] = value.astype(BF16)
    for copy in pz:
        copy.wait_recv()

    back = returned[...].reshape(total, width)
    rest = mix[...]
    result = jnp.zeros((tok_rows, width), F32)
    for _ in range(3):
        piece = rest.astype(BF16)
        rest = rest - piece.astype(F32)
        result += jnp.dot(piece, back, preferred_element_type=F32)
    out_ref[...] = result.astype(BF16)
    for copy in sent:
        copy.wait_send()


def fused_body(tokens, expert_ids, route_weights, w_gate, w_up, w_down):
    experts = lax.axis_size("expert")
    tok_rows, model_width = tokens.shape
    cap = tok_rows * 5 // 8
    width = model_width // PARTS
    units = w_gate.shape[2]
    vmem = pl.BlockSpec(memory_space=pltpu.VMEM)
    hbm = pl.BlockSpec(memory_space=pl.ANY)
    blocks = (experts, cap, width)
    flops = 2 * 3 * experts * cap * model_width * units
    dma = pltpu.SemaphoreType.DMA
    return pl.pallas_call(
        functools.partial(layer_kernel, experts),
        out_shape=jax.ShapeDtypeStruct((tok_rows, width), BF16),
        in_specs=[vmem, vmem, vmem, hbm, hbm, hbm],
        out_specs=vmem,
        scratch_shapes=[
            pltpu.VMEM((model_width, units), BF16),
            pltpu.VMEM((model_width, units), BF16),
            pltpu.VMEM((units, model_width), BF16),
            pltpu.VMEM((PARTS,) + blocks, BF16),
            pltpu.VMEM(blocks, BF16),
            pltpu.VMEM((experts * cap, units), BF16),
            pltpu.VMEM((tok_rows, experts * cap), F32),
            pltpu.VMEM((2,) + blocks, BF16),
            pltpu.VMEM((2,) + blocks, BF16),
            pltpu.VMEM(blocks, F32),
            pltpu.VMEM(blocks, F32),
            pltpu.VMEM(blocks, BF16),
            pltpu.VMEM(blocks, BF16),
            pltpu.VMEM(blocks, BF16),
            pltpu.VMEM(blocks, BF16),
            dma((3, PARTS)),
        ]
        + [dma((experts,))] * 8
        + [dma((2,))] * 2
        + [dma((experts,))] * 4,
        compiler_params=pltpu.CompilerParams(
            collective_id=0, has_side_effects=True, vmem_limit_bytes=60 * 2**20
        ),
        cost_estimate=pl.CostEstimate(
            flops=flops, bytes_accessed=3 * model_width * units * 2, transcendentals=experts * cap * units
        ),
    )(expert_ids, route_weights, tokens, w_gate, w_up, w_down)


def solution(mesh):
    placed = (
        P(("groups", "expert"), None),
        P(("groups", "expert"), None),
        P(("groups", "expert"), None),
        P("expert", None, "etp"),
        P("expert", None, "etp"),
        P("expert", "etp", None),
    )
    body = fused_body if mesh.shape["etp"] == PARTS else wide_body
    return jax.shard_map(
        body, mesh=mesh, in_specs=placed, out_specs=P(("groups", "expert"), "etp"), check_vma=False
    )
```

```python
import functools

import jax
import jax.numpy as jnp
from jax import lax
from jax.experimental import pallas as pl
from jax.experimental.pallas import tpu as pltpu
from jax.sharding import PartitionSpec as P

MESH = pl.DeviceIdType.MESH
F32 = jnp.float32
BF16 = jnp.bfloat16
TILE = 256
WIDE = 1024
PARTS = 4


def route_places(expert_ids, experts, capacity):
    routes_flat = expert_ids.reshape(-1)
    labels = jnp.arange(experts, dtype=jnp.int32)
    matches = (routes_flat[:, None] == labels[None, :]).astype(jnp.int32)
    earlier = jnp.cumsum(matches, axis=0) - matches
    slots = jnp.sum(earlier * matches, axis=1)
    return routes_flat * capacity + slots


def dispatch_rows(source_rows, places, experts, capacity):
    count_rows = source_rows.shape[0]
    targets = jnp.arange(experts * capacity, dtype=jnp.int32)
    matrix = (targets[:, None] == places[None, :]).astype(BF16)
    matrix = matrix.reshape(experts * capacity, count_rows, 2).sum(axis=2)
    placed = jnp.dot(matrix, source_rows, preferred_element_type=F32).astype(BF16)
    return placed.reshape(experts, capacity, source_rows.shape[1])


def wide_body(tokens, expert_ids, route_weights, w_gate, w_up, w_down):
    experts = lax.axis_size("expert")
    shards = lax.axis_size("etp")
    tok_rows = tokens.shape[0]
    capacity = tok_rows * 5 // 8
    model_width = tokens.shape[1]
    slice_width = model_width // shards
    places = route_places(expert_ids, experts, capacity)
    outgoing = dispatch_rows(tokens, places, experts, capacity)
    arrived = lax.all_to_all(outgoing, "expert", split_axis=0, concat_axis=0, tiled=True)
    rows_in = arrived.reshape(experts * capacity, model_width)
    gate_act = jnp.dot(rows_in, w_gate[0], preferred_element_type=F32)
    up_act = jnp.dot(rows_in, w_up[0], preferred_element_type=F32)
    hidden = (jax.nn.silu(gate_act) * up_act).astype(BF16)
    partial_rows = jnp.dot(hidden, w_down[0], preferred_element_type=F32).astype(BF16)
    partial_value = partial_rows.reshape(experts, capacity, model_width)
    expert_out = lax.psum_scatter(partial_value, "etp", scatter_dimension=2, tiled=True)
    returned = lax.all_to_all(expert_out, "expert", split_axis=0, concat_axis=0, tiled=True)
    picked = returned.reshape(experts * capacity, slice_width)[places]
    weighted = picked.astype(F32) * route_weights.reshape(-1)[:, None]
    combined = jnp.sum(weighted.reshape(tok_rows, 2, slice_width), axis=1)
    return combined.astype(BF16)


def layer_kernel(
    experts,
    ids_ref, wts_ref, tok_hbm, gate_hbm, up_hbm, down_hbm,
    out_ref,
    tok_ref, gate, up, down, rows, outgoing, gate_sum, up_sum, hidden, mix,
    core_out, core_in, far_sum, own_sum, x_out, x_in, z_out, returned,
    tok_sem, w_sem, z_send, z_recv, c_send, c_recv, x_send, x_recv, d_send, d_recv,
    pc_send, pc_recv, px_send, px_recv, pz_send, pz_recv,
):
    me = lax.axis_index("etp")
    z = lax.axis_index("expert")
    chip = me // 2
    core = me - chip * 2
    core_peer = chip * 2 + (1 - core)
    x_peer = (1 - chip) * 2 + core
    diagonal = (1 - chip) * 2 + (1 - core)
    tok_rows = tok_ref.shape[0]
    cap = rows.shape[2]
    width = rows.shape[3]
    total = experts * cap
    units = hidden.shape[1]

    tok_copy = pltpu.make_async_copy(tok_hbm, tok_ref, tok_sem)
    tok_copy.start()

    barrier = pltpu.get_barrier_semaphore()
    others = [lax.rem(z + d, experts) for d in range(experts)]
    for d in range(1, experts):
        pl.semaphore_signal(barrier, inc=1, device_id={"expert": others[d]}, device_id_type=MESH)
    for peer in (core_peer, x_peer):
        pl.semaphore_signal(barrier, inc=1, device_id={"etp": peer}, device_id_type=MESH)

    ids = ids_ref[...]
    wts = wts_ref[...]
    label = lax.broadcasted_iota(jnp.int32, (2 * PARTS if experts <= 2 * PARTS else experts, tok_rows), 0)
    match = [ids[k : k + 1] == label for k in range(2)]
    counts = (match[0].astype(F32) + match[1].astype(F32)).astype(BF16)
    row_at = lax.broadcasted_iota(jnp.int32, (tok_rows, tok_rows), 0)
    col_at = lax.broadcasted_iota(jnp.int32, (tok_rows, tok_rows), 1)
    before = (row_at < col_at).astype(F32).astype(BF16)
    earlier = jnp.dot(counts, before, preferred_element_type=F32)
    places = []
    for k in range(2):
        slot = jnp.sum(jnp.where(match[k], earlier, 0.0), axis=0, keepdims=True)
        places.append(ids[k : k + 1] * cap + slot.astype(jnp.int32))
    target = lax.broadcasted_iota(jnp.int32, (total, tok_rows), 0)
    hit = [places[k] == target for k in range(2)]
    spread = (hit[0].astype(F32) + hit[1].astype(F32)).astype(BF16)
    tok_copy.wait()

    down_chunk = down.shape[0] // PARTS
    gate_copies, down_copies = [], []
    for i, q in enumerate((me, core_peer, x_peer, diagonal)):
        at = pl.ds(pl.multiple_of(q * width, width), width)
        gate_copies.append(pltpu.make_async_copy(gate_hbm.at[0, at], gate.at[at], w_sem.at[0, i]))
        gate_copies.append(pltpu.make_async_copy(up_hbm.at[0, at], up.at[at], w_sem.at[1, i]))
    for part in range(PARTS):
        at = slice(part * down_chunk, (part + 1) * down_chunk)
        down_copies.append(pltpu.make_async_copy(down_hbm.at[0, at], down.at[at], w_sem.at[2, part]))
    for copy in gate_copies:
        copy.start()
    my_columns = tok_ref[:, pl.ds(pl.multiple_of(me * width, 128), width)]
    placed = jnp.dot(spread, my_columns, preferred_element_type=F32)
    outgoing[...] = placed.astype(BF16).reshape(experts, cap, width)

    pl.semaphore_wait(barrier, experts + 1)

    def remote(src, dst, send, recv, **device):
        return pltpu.make_async_remote_copy(
            src_ref=src, dst_ref=dst, send_sem=send, recv_sem=recv,
            device_id=device, device_id_type=MESH,
        )

    sent = []

    def go(copy):
        copy.start()
        sent.append(copy)
        return copy

    z_copies = [
        go(remote(outgoing.at[others[d]], rows.at[me, d], z_send.at[d], z_recv.at[d], expert=others[d]))
        for d in range(1, experts)
    ]

    slot_at = lax.broadcasted_iota(jnp.int32, (cap, tok_rows), 0) + z * cap
    own_hit = [places[k] == slot_at for k in range(2)]
    own_spread = (own_hit[0].astype(F32) + own_hit[1].astype(F32)).astype(BF16)
    for q in range(PARTS):
        own = jnp.dot(own_spread, tok_ref[:, q * width : (q + 1) * width], preferred_element_type=F32)
        rows[q, 0] = own.astype(BF16)

    rest = jnp.where(hit[0], wts[0:1], 0.0) + jnp.where(hit[1], wts[1:2], 0.0)
    diagonal_ones = (row_at == col_at).astype(F32).astype(BF16)
    for i in range(3):
        piece = rest.astype(BF16)
        rest = rest - piece.astype(F32)
        turned = lax.dot_general(diagonal_ones, piece, (((1,), (1,)), ((), ())), preferred_element_type=F32)
        mix[i] = turned.astype(BF16)

    def own_part(low, high):
        @pl.loop(low, high)
        def _(n):
            cols = pl.ds(pl.multiple_of(n * WIDE, WIDE), WIDE)
            gate_act = jnp.zeros((cap, WIDE), F32)
            up_act = jnp.zeros((cap, WIDE), F32)
            for q in range(PARTS):
                at = slice(q * width, (q + 1) * width)
                gate_act += jnp.dot(rows[q, 0], gate[at, cols], preferred_element_type=F32)
                up_act += jnp.dot(rows[q, 0], up[at, cols], preferred_element_type=F32)
            hidden[:cap, cols] = (gate_act / (1.0 + jnp.exp(-gate_act)) * up_act).astype(BF16)

    rest_rows = total - cap

    def multiply(q, is_first, is_last):
        @pl.loop(0, units // WIDE)
        def _(n):
            cols = pl.ds(pl.multiple_of(n * WIDE, WIDE), WIDE)
            at = pl.ds(pl.multiple_of(q * width, width), width)
            block = rows[q, 1:].reshape(rest_rows, width)
            gate_act = jnp.dot(block, gate[at, cols], preferred_element_type=F32)
            up_act = jnp.dot(block, up[at, cols], preferred_element_type=F32)
            if not is_first:
                gate_act += gate_sum[:, cols]
                up_act += up_sum[:, cols]
            if is_last:
                hidden[cap:, cols] = (gate_act / (1.0 + jnp.exp(-gate_act)) * up_act).astype(BF16)
            else:
                gate_sum[:, cols] = gate_act
                up_sum[:, cols] = up_act

    c_copies, x_copies, d_copies = [], [], []
    for d in range(1, experts):
        z_copies[d - 1].wait_recv()
        block = rows.at[me, d]
        x_copies.append(go(remote(block, block, x_send.at[d], x_recv.at[d], etp=x_peer)))
        c_copies.append(go(remote(block, block, c_send.at[d], c_recv.at[d], etp=core_peer)))
        if d == 1:
            for copy in gate_copies:
                copy.wait()
            for copy in down_copies:
                copy.start()
            own_part(0, units // WIDE // 2)
        if d == 2:
            own_part(units // WIDE // 2, units // WIDE)

    def pass_on(d):
        x_copies[d - 1].wait_recv()
        block = rows.at[x_peer, d]
        d_copies.append(go(remote(block, block, d_send.at[d], d_recv.at[d], etp=core_peer)))

    multiply(me, True, False)
    for d in range(1, experts - 1):
        pass_on(d)
    for copy in c_copies:
        copy.wait_recv()
    multiply(core_peer, False, False)
    pass_on(experts - 1)
    multiply(x_peer, False, False)
    for copy in d_copies:
        copy.wait_recv()
    multiply(diagonal, False, True)

    for copy in down_copies:
        copy.wait()

    def project(q, target_ref):
        @pl.loop(0, width // TILE)
        def _(n):
            start = pl.multiple_of(n * TILE, TILE)
            cols = pl.ds(pl.multiple_of(q * width + n * TILE, TILE), TILE)
            value = jnp.dot(hidden[...], down[:, cols], preferred_element_type=F32)
            target_ref[:, :, pl.ds(start, TILE)] = value.reshape(experts, cap, TILE).astype(target_ref.dtype)

    project(diagonal, core_out.at[0])
    first = go(remote(core_out.at[0], core_in.at[0], pc_send.at[0], pc_recv.at[0], etp=core_peer))
    project(x_peer, far_sum)
    first.wait_recv()
    px = []
    order = list(range(1, experts)) + [0]
    for i, block in enumerate(order):
        x_out[block] = (far_sum[block] + core_in[0, block].astype(F32)).astype(BF16)
        px.append(go(remote(x_out.at[block], x_in.at[block], px_send.at[i], px_recv.at[i], etp=x_peer)))
    project(core_peer, core_out.at[1])
    second = go(remote(core_out.at[1], core_in.at[1], pc_send.at[1], pc_recv.at[1], etp=core_peer))
    project(me, own_sum)
    second.wait_recv()

    pz = []
    for i, block in enumerate(order):
        px[i].wait_recv()
        value = own_sum[block] + core_in[1, block].astype(F32) + x_in[block].astype(F32)
        if i < experts - 1:
            z_out[block] = value.astype(BF16)
            pz.append(go(remote(z_out.at[block], returned.at[z], pz_send.at[i], pz_recv.at[i], expert=lax.rem(z + experts - block, experts))))
        else:
            returned[z] = value.astype(BF16)
    for copy in pz:
        copy.wait_recv()

    back = returned[...].reshape(total, width)
    result = jnp.zeros((tok_rows, width), F32)
    for i in range(3):
        result += jnp.dot(mix[i], back, preferred_element_type=F32)
    out_ref[...] = result
    for copy in sent:
        copy.wait_send()


def fused_body(tokens, expert_ids, route_weights, w_gate, w_up, w_down):
    experts = lax.axis_size("expert")
    tok_rows, model_width = tokens.shape
    cap = tok_rows * 5 // 8
    width = model_width // PARTS
    units = w_gate.shape[2]
    vmem = pl.BlockSpec(memory_space=pltpu.VMEM)
    hbm = pl.BlockSpec(memory_space=pl.ANY)
    blocks = (experts, cap, width)
    flops = 2 * 3 * experts * cap * model_width * units
    dma = pltpu.SemaphoreType.DMA
    return pl.pallas_call(
        functools.partial(layer_kernel, experts),
        out_shape=jax.ShapeDtypeStruct((tok_rows, width), F32),
        in_specs=[vmem, vmem, hbm, hbm, hbm, hbm],
        out_specs=vmem,
        scratch_shapes=[
            pltpu.VMEM((tok_rows, model_width), BF16),
            pltpu.VMEM((model_width, units), BF16),
            pltpu.VMEM((model_width, units), BF16),
            pltpu.VMEM((units, model_width), BF16),
            pltpu.VMEM((PARTS,) + blocks, BF16),
            pltpu.VMEM(blocks, BF16),
            pltpu.VMEM(((experts - 1) * cap, units), F32),
            pltpu.VMEM(((experts - 1) * cap, units), F32),
            pltpu.VMEM((experts * cap, units), BF16),
            pltpu.VMEM((3, tok_rows, experts * cap), BF16),
            pltpu.VMEM((2,) + blocks, BF16),
            pltpu.VMEM((2,) + blocks, BF16),
            pltpu.VMEM(blocks, F32),
            pltpu.VMEM(blocks, F32),
            pltpu.VMEM(blocks, BF16),
            pltpu.VMEM(blocks, BF16),
            pltpu.VMEM(blocks, BF16),
            pltpu.VMEM(blocks, BF16),
            dma,
            dma((3, PARTS)),
        ]
        + [dma((experts,))] * 8
        + [dma((2,))] * 2
        + [dma((experts,))] * 4,
        compiler_params=pltpu.CompilerParams(
            collective_id=0, has_side_effects=True, vmem_limit_bytes=60 * 2**20
        ),
        cost_estimate=pl.CostEstimate(
            flops=flops, bytes_accessed=3 * model_width * units * 2, transcendentals=experts * cap * units
        ),
    )(expert_ids.T, route_weights.T, tokens, w_gate, w_up, w_down).astype(BF16)


def solution(mesh):
    placed = (
        P(("groups", "expert"), None),
        P(("groups", "expert"), None),
        P(("groups", "expert"), None),
        P("expert", None, "etp"),
        P("expert", None, "etp"),
        P("expert", "etp", None),
    )
    body = fused_body if mesh.shape["etp"] == PARTS else wide_body
    return jax.shard_map(
        body, mesh=mesh, in_specs=placed, out_specs=P(("groups", "expert"), "etp"), check_vma=False
    )
```

```python
import functools

import jax
import jax.numpy as jnp
from jax import lax
from jax.experimental import pallas as pl
from jax.experimental.pallas import tpu as pltpu
from jax.sharding import PartitionSpec as P

MESH = pl.DeviceIdType.MESH
F32 = jnp.float32
BF16 = jnp.bfloat16
TILE = 256
WIDE = 1024
PARTS = 4


def route_places(expert_ids, experts, capacity):
    routes_flat = expert_ids.reshape(-1)
    labels = jnp.arange(experts, dtype=jnp.int32)
    matches = (routes_flat[:, None] == labels[None, :]).astype(jnp.int32)
    earlier = jnp.cumsum(matches, axis=0) - matches
    slots = jnp.sum(earlier * matches, axis=1)
    return routes_flat * capacity + slots


def dispatch_rows(source_rows, places, experts, capacity):
    count_rows = source_rows.shape[0]
    targets = jnp.arange(experts * capacity, dtype=jnp.int32)
    matrix = (targets[:, None] == places[None, :]).astype(BF16)
    matrix = matrix.reshape(experts * capacity, count_rows, 2).sum(axis=2)
    placed = jnp.dot(matrix, source_rows, preferred_element_type=F32).astype(BF16)
    return placed.reshape(experts, capacity, source_rows.shape[1])


def wide_body(tokens, expert_ids, route_weights, w_gate, w_up, w_down):
    experts = lax.axis_size("expert")
    shards = lax.axis_size("etp")
    tok_rows = tokens.shape[0]
    capacity = tok_rows * 5 // 8
    model_width = tokens.shape[1]
    slice_width = model_width // shards
    places = route_places(expert_ids, experts, capacity)
    outgoing = dispatch_rows(tokens, places, experts, capacity)
    arrived = lax.all_to_all(outgoing, "expert", split_axis=0, concat_axis=0, tiled=True)
    rows_in = arrived.reshape(experts * capacity, model_width)
    gate_act = jnp.dot(rows_in, w_gate[0], preferred_element_type=F32)
    up_act = jnp.dot(rows_in, w_up[0], preferred_element_type=F32)
    hidden = (jax.nn.silu(gate_act) * up_act).astype(BF16)
    partial_rows = jnp.dot(hidden, w_down[0], preferred_element_type=F32).astype(BF16)
    partial_value = partial_rows.reshape(experts, capacity, model_width)
    expert_out = lax.psum_scatter(partial_value, "etp", scatter_dimension=2, tiled=True)
    returned = lax.all_to_all(expert_out, "expert", split_axis=0, concat_axis=0, tiled=True)
    picked = returned.reshape(experts * capacity, slice_width)[places]
    weighted = picked.astype(F32) * route_weights.reshape(-1)[:, None]
    combined = jnp.sum(weighted.reshape(tok_rows, 2, slice_width), axis=1)
    return combined.astype(BF16)


def layer_kernel(
    experts,
    ids_ref, wts_ref, tok_hbm, gate_hbm, up_hbm, down_hbm,
    out_ref,
    tok_ref, gate, up, down, rows, outgoing, gate_sum, up_sum, hidden, mix,
    core_out, core_in, far_sum, own_sum, x_out, x_in, z_out, returned,
    tok_sem, w_sem, z_send, z_recv, c_send, c_recv, x_send, x_recv, d_send, d_recv,
    pc_send, pc_recv, px_send, px_recv, pz_send, pz_recv,
):
    me = lax.axis_index("etp")
    z = lax.axis_index("expert")
    chip = me // 2
    core = me - chip * 2
    core_peer = chip * 2 + (1 - core)
    x_peer = (1 - chip) * 2 + core
    diagonal = (1 - chip) * 2 + (1 - core)
    tok_rows = tok_ref.shape[0]
    cap = rows.shape[2]
    width = rows.shape[3]
    total = experts * cap
    units = hidden.shape[1]

    tok_copy = pltpu.make_async_copy(tok_hbm, tok_ref, tok_sem)
    tok_copy.start()

    barrier = pltpu.get_barrier_semaphore()
    others = [lax.rem(z + d, experts) for d in range(experts)]
    for d in range(1, experts):
        pl.semaphore_signal(barrier, inc=1, device_id={"expert": others[d]}, device_id_type=MESH)
    for peer in (core_peer, x_peer):
        pl.semaphore_signal(barrier, inc=1, device_id={"etp": peer}, device_id_type=MESH)

    ids = ids_ref[...]
    wts = wts_ref[...]
    label = lax.broadcasted_iota(jnp.int32, (2 * PARTS if experts <= 2 * PARTS else experts, tok_rows), 0)
    match = [ids[k : k + 1] == label for k in range(2)]
    counts = (match[0].astype(F32) + match[1].astype(F32)).astype(BF16)
    row_at = lax.broadcasted_iota(jnp.int32, (tok_rows, tok_rows), 0)
    col_at = lax.broadcasted_iota(jnp.int32, (tok_rows, tok_rows), 1)
    before = (row_at < col_at).astype(F32).astype(BF16)
    earlier = jnp.dot(counts, before, preferred_element_type=F32)
    places = []
    for k in range(2):
        slot = jnp.sum(jnp.where(match[k], earlier, 0.0), axis=0, keepdims=True)
        places.append(ids[k : k + 1] * cap + slot.astype(jnp.int32))
    target = lax.broadcasted_iota(jnp.int32, (total, tok_rows), 0)
    hit = [places[k] == target for k in range(2)]
    spread = (hit[0].astype(F32) + hit[1].astype(F32)).astype(BF16)
    tok_copy.wait()

    down_chunk = down.shape[0] // PARTS
    gate_copies, down_copies = [], []
    for i, q in enumerate((me, core_peer, x_peer, diagonal)):
        at = pl.ds(pl.multiple_of(q * width, width), width)
        gate_copies.append(pltpu.make_async_copy(gate_hbm.at[0, at], gate.at[at], w_sem.at[0, i]))
        gate_copies.append(pltpu.make_async_copy(up_hbm.at[0, at], up.at[at], w_sem.at[1, i]))
    for part in range(PARTS):
        at = slice(part * down_chunk, (part + 1) * down_chunk)
        down_copies.append(pltpu.make_async_copy(down_hbm.at[0, at], down.at[at], w_sem.at[2, part]))
    for copy in gate_copies:
        copy.start()
    my_columns = tok_ref[:, pl.ds(pl.multiple_of(me * width, 128), width)]
    placed = jnp.dot(spread, my_columns, preferred_element_type=F32)
    outgoing[...] = placed.astype(BF16).reshape(experts, cap, width)

    pl.semaphore_wait(barrier, experts + 1)

    def remote(src, dst, send, recv, **device):
        return pltpu.make_async_remote_copy(
            src_ref=src, dst_ref=dst, send_sem=send, recv_sem=recv,
            device_id=device, device_id_type=MESH,
        )

    sent = []

    def go(copy):
        copy.start()
        sent.append(copy)
        return copy

    z_copies = [
        go(remote(outgoing.at[others[d]], rows.at[me, d], z_send.at[d], z_recv.at[d], expert=others[d]))
        for d in range(1, experts)
    ]

    slot_at = lax.broadcasted_iota(jnp.int32, (cap, tok_rows), 0) + z * cap
    own_hit = [places[k] == slot_at for k in range(2)]
    own_spread = (own_hit[0].astype(F32) + own_hit[1].astype(F32)).astype(BF16)
    for q in range(PARTS):
        own = jnp.dot(own_spread, tok_ref[:, q * width : (q + 1) * width], preferred_element_type=F32)
        rows[q, 0] = own.astype(BF16)

    rest = jnp.where(hit[0], wts[0:1], 0.0) + jnp.where(hit[1], wts[1:2], 0.0)
    diagonal_ones = (row_at == col_at).astype(F32).astype(BF16)
    for i in range(3):
        piece = rest.astype(BF16)
        rest = rest - piece.astype(F32)
        turned = lax.dot_general(diagonal_ones, piece, (((1,), (1,)), ((), ())), preferred_element_type=F32)
        mix[i] = turned.astype(BF16)

    def own_part(low, high):
        @pl.loop(low, high)
        def _(n):
            cols = pl.ds(pl.multiple_of(n * WIDE, WIDE), WIDE)
            gate_act = jnp.zeros((cap, WIDE), F32)
            up_act = jnp.zeros((cap, WIDE), F32)
            for q in range(PARTS):
                at = slice(q * width, (q + 1) * width)
                gate_act += jnp.dot(rows[q, 0], gate[at, cols], preferred_element_type=F32)
                up_act += jnp.dot(rows[q, 0], up[at, cols], preferred_element_type=F32)
            hidden[:cap, cols] = (gate_act / (1.0 + jnp.exp(-gate_act)) * up_act).astype(BF16)

    rest_rows = total - cap

    def multiply(q, is_first, is_last):
        @pl.loop(0, units // WIDE)
        def _(n):
            cols = pl.ds(pl.multiple_of(n * WIDE, WIDE), WIDE)
            at = pl.ds(pl.multiple_of(q * width, width), width)
            block = rows[q, 1:].reshape(rest_rows, width)
            gate_act = jnp.dot(block, gate[at, cols], preferred_element_type=F32)
            up_act = jnp.dot(block, up[at, cols], preferred_element_type=F32)
            if not is_first:
                gate_act += gate_sum[:, cols]
                up_act += up_sum[:, cols]
            if is_last:
                hidden[cap:, cols] = (gate_act / (1.0 + jnp.exp(-gate_act)) * up_act).astype(BF16)
            else:
                gate_sum[:, cols] = gate_act
                up_sum[:, cols] = up_act

    c_copies, x_copies, d_copies = [], [], []
    for d in range(1, experts):
        z_copies[d - 1].wait_recv()
        block = rows.at[me, d]
        x_copies.append(go(remote(block, block, x_send.at[d], x_recv.at[d], etp=x_peer)))
        c_copies.append(go(remote(block, block, c_send.at[d], c_recv.at[d], etp=core_peer)))
        if d == 1:
            for copy in gate_copies:
                copy.wait()
            for copy in down_copies:
                copy.start()
            own_part(0, units // WIDE // 2)
        if d == 2:
            own_part(units // WIDE // 2, units // WIDE)

    def pass_on(d):
        x_copies[d - 1].wait_recv()
        block = rows.at[x_peer, d]
        d_copies.append(go(remote(block, block, d_send.at[d], d_recv.at[d], etp=core_peer)))

    multiply(me, True, False)
    for d in range(1, experts - 1):
        pass_on(d)
    for copy in c_copies:
        copy.wait_recv()
    multiply(core_peer, False, False)
    pass_on(experts - 1)
    multiply(x_peer, False, False)
    for copy in d_copies:
        copy.wait_recv()
    multiply(diagonal, False, True)

    for copy in down_copies:
        copy.wait()

    def project(q, target_ref):
        @pl.loop(0, width // TILE)
        def _(n):
            start = pl.multiple_of(n * TILE, TILE)
            cols = pl.ds(pl.multiple_of(q * width + n * TILE, TILE), TILE)
            value = jnp.dot(hidden[...], down[:, cols], preferred_element_type=F32)
            target_ref[:, :, pl.ds(start, TILE)] = value.reshape(experts, cap, TILE).astype(target_ref.dtype)

    project(diagonal, core_out.at[0])
    first = go(remote(core_out.at[0], core_in.at[0], pc_send.at[0], pc_recv.at[0], etp=core_peer))
    project(x_peer, far_sum)
    first.wait_recv()
    px = []
    middle = experts // 2
    order = [middle] + [d for d in range(1, experts) if d != middle] + [0]
    for i, block in enumerate(order):
        x_out[block] = (far_sum[block] + core_in[0, block].astype(F32)).astype(BF16)
        px.append(go(remote(x_out.at[block], x_in.at[block], px_send.at[i], px_recv.at[i], etp=x_peer)))
    project(core_peer, core_out.at[1])
    second = go(remote(core_out.at[1], core_in.at[1], pc_send.at[1], pc_recv.at[1], etp=core_peer))
    project(me, own_sum)
    second.wait_recv()

    pz = []
    for i, block in enumerate(order):
        px[i].wait_recv()
        value = own_sum[block] + core_in[1, block].astype(F32) + x_in[block].astype(F32)
        if i < experts - 1:
            z_out[block] = value.astype(BF16)
            pz.append(go(remote(z_out.at[block], returned.at[z], pz_send.at[i], pz_recv.at[i], expert=lax.rem(z + experts - block, experts))))
        else:
            returned[z] = value.astype(BF16)
    for copy in pz:
        copy.wait_recv()

    back = returned[...].reshape(total, width)
    result = jnp.zeros((tok_rows, width), F32)
    for i in range(3):
        result += jnp.dot(mix[i], back, preferred_element_type=F32)
    out_ref[...] = result
    for copy in sent:
        copy.wait_send()


def fused_body(tokens, expert_ids, route_weights, w_gate, w_up, w_down):
    experts = lax.axis_size("expert")
    tok_rows, model_width = tokens.shape
    cap = tok_rows * 5 // 8
    width = model_width // PARTS
    units = w_gate.shape[2]
    vmem = pl.BlockSpec(memory_space=pltpu.VMEM)
    hbm = pl.BlockSpec(memory_space=pl.ANY)
    blocks = (experts, cap, width)
    flops = 2 * 3 * experts * cap * model_width * units
    dma = pltpu.SemaphoreType.DMA
    return pl.pallas_call(
        functools.partial(layer_kernel, experts),
        out_shape=jax.ShapeDtypeStruct((tok_rows, width), F32),
        in_specs=[vmem, vmem, hbm, hbm, hbm, hbm],
        out_specs=vmem,
        scratch_shapes=[
            pltpu.VMEM((tok_rows, model_width), BF16),
            pltpu.VMEM((model_width, units), BF16),
            pltpu.VMEM((model_width, units), BF16),
            pltpu.VMEM((units, model_width), BF16),
            pltpu.VMEM((PARTS,) + blocks, BF16),
            pltpu.VMEM(blocks, BF16),
            pltpu.VMEM(((experts - 1) * cap, units), F32),
            pltpu.VMEM(((experts - 1) * cap, units), F32),
            pltpu.VMEM((experts * cap, units), BF16),
            pltpu.VMEM((3, tok_rows, experts * cap), BF16),
            pltpu.VMEM((2,) + blocks, BF16),
            pltpu.VMEM((2,) + blocks, BF16),
            pltpu.VMEM(blocks, F32),
            pltpu.VMEM(blocks, F32),
            pltpu.VMEM(blocks, BF16),
            pltpu.VMEM(blocks, BF16),
            pltpu.VMEM(blocks, BF16),
            pltpu.VMEM(blocks, BF16),
            dma,
            dma((3, PARTS)),
        ]
        + [dma((experts,))] * 8
        + [dma((2,))] * 2
        + [dma((experts,))] * 4,
        compiler_params=pltpu.CompilerParams(
            collective_id=0, has_side_effects=True, vmem_limit_bytes=60 * 2**20
        ),
        cost_estimate=pl.CostEstimate(
            flops=flops, bytes_accessed=3 * model_width * units * 2, transcendentals=experts * cap * units
        ),
    )(expert_ids.T, route_weights.T, tokens, w_gate, w_up, w_down).astype(BF16)


def solution(mesh):
    placed = (
        P(("groups", "expert"), None),
        P(("groups", "expert"), None),
        P(("groups", "expert"), None),
        P("expert", None, "etp"),
        P("expert", None, "etp"),
        P("expert", "etp", None),
    )
    body = fused_body if mesh.shape["etp"] == PARTS else wide_body
    return jax.shard_map(
        body, mesh=mesh, in_specs=placed, out_specs=P(("groups", "expert"), "etp"), check_vma=False
    )
```
